128 devices in a mesh: section: 4 (over z_lo, core), seq: 32 (over z_hi, y, x).
Axes of the slice: x: 4, y: 4, z: 4 (z_hi: 2, z_lo: 2; z = z_hi * 2 + z_lo), core: 2. Of those that a mesh axis runs over, the one named last changes fastest.
Arguments:
- tokens: bfloat16 [4, 1024, 6144], P('section', 'seq'), may hold values from -6 to 6
- mod_shift: float32 [4, 6144], P('section'), may hold values from -0.5 to 0.5
- mod_scale: float32 [4, 6144], P('section'), may hold values from -0.5 to 0.5
- mod_gate: float32 [4, 6144], P('section'), may hold values from 0.5 to 1.5
- w_query: bfloat16 [4, 6144, 4096], P('section', None, 'seq'), may hold values from -1 to 1
- w_key: bfloat16 [4, 6144, 4096], P('section', None, 'seq'), may hold values from -0.078125 to 0.078125
- w_value: bfloat16 [4, 6144, 4096], P('section', None, 'seq'), may hold values from -0.078125 to 0.078125
- w_out: bfloat16 [4, 4096, 6144], P('section', 'seq'), may hold values from -0.09375 to 0.09375
- stale_keys: bfloat16 [4, 13312, 4096], P('section', 'seq'), may hold values from -410 to 410
- stale_values: bfloat16 [4, 13312, 4096], P('section', 'seq'), may hold values from -6 to 6
- patch_index: int32 [4], P('section'), may hold values from 0 to 12
Outputs:
- forwarded: bfloat16 [4, 1024, 6144], P('section', 'seq')
The draws below stay inside these ranges and needn't reach their ends.
All inputs are finite; a program needn't handle non-finite values.
Results may differ from the reference program's by a relative error of at most 0.011.
Values may be sent and summed in bfloat16 or wider, within the bound.
No kernel may reach another device: no remote copies, remote signals or barrier semaphores. Data moves between devices by JAX's collectives and lax.ppermute only.
A program may use at most 192 MiB of HBM per device.

```python
import jax
import jax.numpy as jnp
from jax import lax

D = 6144
HD = 128
HEADS = 32
INNER = 4096
PATCH = 1024
NPATCH = 13
SEQ = 13312
SECTIONS = 4


def query_weights(key):
    weight_key = jax.random.fold_in(key, 5102)
    raw = jax.random.normal(weight_key, (SECTIONS, D, INNER), jnp.float32)
    return jnp.clip(raw, -4.0, 4.0) * D ** (-0.5)


def draw_w_query(key, part):
    return query_weights(key).astype(jnp.bfloat16)


def draw_tokens(key, part):
    own = jax.random.fold_in(key, 31)
    return jnp.clip(jax.random.normal(own, (SECTIONS, PATCH, D), jnp.float32), -6.0, 6.0).astype(jnp.bfloat16)


def draw_stale_keys(key, part):
    own = jax.random.fold_in(key, 37)
    return jnp.clip(jax.random.normal(own, (SECTIONS, SEQ, INNER), jnp.float32), -6.0, 6.0).astype(jnp.bfloat16)


def set_ends(entries, own_key, smallest, top_value):
    longest = entries.shape.index(max(entries.shape))
    spots = []
    for shift in (0, 1):
        where = [jax.random.randint(jax.random.fold_in(own_key, axis), (), 0, length) for axis, length in enumerate(entries.shape)]
        where[longest] = (where[longest] + shift) % entries.shape[longest]
        spots.append(tuple(where))
    return entries.at[spots[0]].set(smallest).at[spots[1]].set(top_value)


def block_scale(stream_key, dims, pieces, least, top_value):
    def one(position, shards_of):
        draws = jax.random.uniform(jax.random.fold_in(jax.random.fold_in(stream_key, 6), position), (shards_of,), jnp.float32, least / len(pieces), top_value / len(pieces))
        return jnp.repeat(jnp.exp(draws), dims[position] // shards_of).reshape((-1,) + (1,) * (len(dims) - position - 1))

    gain = one(*pieces[0])
    for cut in pieces[1:]:
        gain = gain * one(*cut)
    return gain


def noise(own_key, dims, scale, bound, cuts=(), held_as=jnp.bfloat16):
    values = jax.random.normal(own_key, dims, jnp.float32) * scale
    if len(cuts) > 0:
        values = block_scale(own_key, dims, cuts, -0.22, 0.18) * values
    return jnp.clip(values, min=-bound, max=bound).astype(held_as)


def setup_inputs(seed: int = 0) -> dict:
    key_list = jax.random.split(jax.random.key(seed), 12)
    return {
        "tokens": draw_tokens(jax.random.fold_in(key_list[11], 71), 0),
        "mod_shift": jnp.clip(jax.random.uniform(key_list[1], (SECTIONS, D), jnp.float32, -0.5, 0.5) * block_scale(key_list[1], (SECTIONS, D), ((0, 4),), -0.4, 0.0), -0.5, 0.5),
        "mod_scale": jnp.clip(jax.random.uniform(key_list[2], (SECTIONS, D), jnp.float32, -0.5, 0.5) * block_scale(key_list[2], (SECTIONS, D), ((0, 4),), -0.4, 0.0), -0.5, 0.5),
        "mod_gate": jnp.clip(0.5 + 1.0 * jax.random.uniform(key_list[3], (SECTIONS, D), jnp.float32) ** block_scale(key_list[3], (SECTIONS, D), ((0, 4),), -0.2, 0.2), 0.5, 1.5),
        "w_query": draw_w_query(jax.random.fold_in(key_list[11], 71), 0),
        "w_key": noise(key_list[5], (SECTIONS, D, INNER), D ** -0.5, 0.078125, ((0, 4), (2, 32))),
        "w_value": noise(key_list[6], (SECTIONS, D, INNER), D ** -0.5, 0.078125, ((0, 4), (2, 32))),
        "w_out": noise(key_list[7], (SECTIONS, INNER, D), INNER ** -0.5, 0.09375, ((0, 4), (1, 32))),
        "stale_keys": draw_stale_keys(jax.random.fold_in(key_list[11], 71), 0),
        "stale_values": noise(key_list[9], (SECTIONS, SEQ, INNER), 1.0, 6.0, ((0, 4), (1, 32))),
        "patch_index": set_ends(jax.random.randint(key_list[10], (SECTIONS,), 0, NPATCH), jax.random.fold_in(key_list[10], 1), 0, NPATCH - 1).astype(jnp.int32),
    }


def head_attention(query, keys, values):
    scores = jnp.dot(query.astype(jnp.float32), keys.astype(jnp.float32).T) / jnp.sqrt(jnp.float32(HD))
    probs = jax.nn.softmax(scores, axis=-1).astype(jnp.bfloat16)
    return jnp.dot(probs.astype(jnp.float32), values.astype(jnp.float32)).astype(jnp.bfloat16)

def reference(tokens, mod_shift, mod_scale, mod_gate, w_query, w_key, w_value, w_out, stale_keys, stale_values, patch_index):
    results = []
    for section in range(SECTIONS):
        inputs = tokens[section].astype(jnp.float32)
        meansq = lax.optimization_barrier(jnp.mean(inputs * inputs, axis=-1, keepdims=True))
        normed = (inputs * lax.rsqrt(meansq + 1e-06) * (1.0 + mod_scale[section]) + mod_shift[section]).astype(jnp.bfloat16)
        query = jnp.dot(normed, w_query[section], preferred_element_type=jnp.float32).astype(jnp.bfloat16)
        keyed = jnp.dot(normed, w_key[section], preferred_element_type=jnp.float32).astype(jnp.bfloat16)
        valued = jnp.dot(normed, w_value[section], preferred_element_type=jnp.float32).astype(jnp.bfloat16)
        offset = (patch_index[section] * PATCH).astype(jnp.int32)
        anchor = jnp.zeros((), jnp.int32)
        all_keys = lax.dynamic_update_slice(stale_keys[section], keyed, (offset, anchor))
        all_values = lax.dynamic_update_slice(stale_values[section], valued, (offset, anchor))
        query_heads = query.reshape(PATCH, HEADS, HD).transpose(1, 0, 2)
        key_heads = all_keys.reshape(SEQ, HEADS, HD).transpose(1, 0, 2)
        value_heads = all_values.reshape(SEQ, HEADS, HD).transpose(1, 0, 2)
        attended = lax.map(lambda trio: head_attention(trio[0], trio[1], trio[2]), (query_heads, key_heads, value_heads))
        attended = attended.transpose(1, 0, 2).reshape(PATCH, INNER)
        projected = jnp.dot(attended, w_out[section], preferred_element_type=jnp.float32)
        results.append((inputs + mod_gate[section] * projected).astype(jnp.bfloat16))
    updated = jnp.stack(results, axis=0)
    return jnp.roll(updated, 1, axis=0)
```

```python
import functools

import jax
import jax.numpy as jnp
from jax import lax
from jax.experimental import pallas as pl
from jax.experimental.pallas import tpu as pltpu
from jax.sharding import PartitionSpec as P

HD = 128
NZ, NY, NX = 2, 4, 4
COUNT = NZ * NY * NX
PLANE = NY * NX
LOG2E = 1.4426950408889634
LOWEST = -1e30
BF = jnp.bfloat16
F32 = jnp.float32


def moved(value, dz=0, dy=0, dx=0):
    pairs = []
    for source in range(COUNT):
        z, y, x = source // PLANE, source // NX % NY, source % NX
        target = (z + dz) % NZ * PLANE + (y + dy) % NY * NX + (x + dx) % NX
        pairs.append((source, target))
    return lax.ppermute(value, "seq", pairs)


def onward(value, sections, dx):
    pairs = []
    for section in range(sections):
        for source in range(COUNT):
            target = source // NX * NX + (source % NX + dx) % NX
            pairs.append((section * COUNT + source, (section + 1) % sections * COUNT + target))
    return lax.ppermute(value, ("section", "seq"), pairs)


def from_behind(value, axis, steps):
    count = lax.axis_size(axis)
    pairs = [(source, (source + steps) % count) for source in range(count)]
    return lax.ppermute(value, axis, pairs)


def after(value, *others):
    return lax.optimization_barrier((value,) + others)[0]


def project_kernel(spot, *refs, pieces, rows):
    block_refs = refs[: len(pieces)]
    w_ref, q_ref, kv_ref, out_ref, x_ref = refs[len(pieces) :]
    z, y, x = spot[0], spot[1], spot[2]
    for ref, (column, steps) in zip(block_refs, pieces):
        wide = ref.shape[-1]
        for at, (dy, dx) in enumerate(steps):
            for plane in range(NZ):
                row = plane * PLANE * rows + lax.rem(y + NY - dy, NY) * NX * rows + lax.rem(x + NX - dx, NX) * rows
                x_ref[pl.ds(pl.multiple_of(row, rows), rows), column : column + wide] = ref[at, plane * rows : (plane + 1) * rows, :]
    half = PLANE * rows
    tile = half // 2

    def step(t, carry):
        start = pl.multiple_of(t * tile, tile)
        part = jnp.dot(x_ref[pl.ds(start, tile), :], w_ref[...], preferred_element_type=F32)
        for head in range(2):
            q = part[:, head * 3 * HD : head * 3 * HD + HD]
            q_ref[head, pl.ds(start, tile), :] = q
            out_ref[head, pl.ds(start, tile), :] = q.astype(BF)
        inner = pl.multiple_of(lax.rem(t, 2) * tile, tile)
        kept = t // 2 == z
        for head in range(2):
            for which in range(2):
                part_kv = part[:, (head * 3 + 1 + which) * HD : (head * 3 + 2 + which) * HD]

                @pl.when(kept)
                def _():
                    kv_ref[which * 2 + head, pl.ds(inner, tile), :] = part_kv

                @pl.when(jnp.logical_not(kept))
                def _():
                    out_ref[2 + which, pl.ds(pl.multiple_of(head * half + inner, tile), tile), :] = part_kv.astype(BF)

        return carry

    lax.fori_loop(0, 4, step, 0)


def project(spot, blocks, pieces, weights, rows):
    depth = weights.shape[0]
    patch = COUNT * rows
    vmem = pl.BlockSpec(memory_space=pltpu.VMEM)
    return pl.pallas_call(
        functools.partial(project_kernel, pieces=pieces, rows=rows),
        out_shape=(
            jax.ShapeDtypeStruct((2, patch, HD), F32),
            jax.ShapeDtypeStruct((4, patch // 2, HD), F32),
            jax.ShapeDtypeStruct((4, patch, HD), BF),
        ),
        in_specs=[pl.BlockSpec(memory_space=pltpu.SMEM)] + [vmem] * (len(blocks) + 1),
        out_specs=(vmem, vmem, vmem),
        scratch_shapes=[pltpu.VMEM((patch, depth), BF)],
        compiler_params=pltpu.CompilerParams(vmem_limit_bytes=44 * 2**20),
        cost_estimate=pl.CostEstimate(
            flops=2 * patch * depth * 6 * HD, bytes_accessed=2 * depth * (patch + 6 * HD) + 6 * patch * HD * 4, transcendentals=0
        ),
    )(spot, *blocks, weights)


def attend_kernel(lows, *refs, fresh, groups, first, last, length, patch):
    refs = list(refs)
    q_ref = refs.pop(0)
    if fresh:
        fresh_k, fresh_v = refs.pop(0), refs.pop(0)
    chunks = sum(groups)
    k_refs, v_refs = refs[:chunks], refs[chunks : 2 * chunks]
    refs = refs[2 * chunks :]
    if not first:
        acc_in, m_in, l_in = refs[:3]
        refs = refs[3:]
    if last:
        o_ref, lse_ref = refs[:2]
    else:
        acc_out, m_out, l_out = refs[:3]
    k_all, v_all, acc, m, l = refs[2 if last else 3 :]

    @pl.when(pl.program_id(1) == 0)
    def _():
        for at in range(chunks):
            k_all[at * length : (at + 1) * length, :] = k_refs[at][0]
            v_all[at * length : (at + 1) * length, :] = v_refs[at][0]

    if first:
        m[...] = jnp.full(m.shape, LOWEST, F32)
        l[...] = jnp.zeros(l.shape, F32)
        acc[...] = jnp.zeros(acc.shape, F32)
    else:
        m[...] = m_in[0]
        l[...] = l_in[0]
        acc[...] = acc_in[0]
    q = q_ref[0]
    scale = LOG2E / HD**0.5

    def update(keys, values, gone):
        s = lax.dot_general(q, keys, (((1,), (1,)), ((), ())), preferred_element_type=F32) * scale
        if gone is not None:
            s = jnp.where(gone, LOWEST, s)
        m_old = m[...]
        m_new = jnp.maximum(m_old, jnp.max(s, axis=1, keepdims=True))
        p = jnp.exp2(s - m_new[:, :1])
        alpha = jnp.exp2(m_old - m_new)
        l[...] = alpha * l[...] + jnp.sum(p, axis=1, keepdims=True)
        acc[...] = alpha * acc[...] + jnp.dot(p.astype(BF), values, preferred_element_type=F32)
        m[...] = m_new

    if fresh:
        update(fresh_k[0], fresh_v[0], None)
    base = 0
    for group in groups:
        size = group * length
        start = base * length
        touched = jnp.bool_(False)
        for at in range(group):
            low = lows[base + at]
            touched = touched | ((low < length) & (low + patch > 0))

        @pl.when(touched)
        def _():
            column = lax.broadcasted_iota(jnp.int32, (1, size), 1)
            gone = jnp.zeros((1, size), jnp.int32)
            for at in range(group):
                low = lows[base + at]
                begin = at * length + jnp.clip(low, 0, length)
                end = at * length + jnp.clip(low + patch, 0, length)
                gone = jnp.where((column >= begin) & (column < end), 1, gone)
            update(k_all[start : start + size, :], v_all[start : start + size, :], gone > 0)

        @pl.when(jnp.logical_not(touched))
        def _():
            update(k_all[start : start + size, :], v_all[start : start + size, :], None)

        base += group
    if last:
        o_ref[0] = acc[...] / l[...]
        lse = m[...] + jnp.log2(l[...])
        lse_ref[0] = jnp.transpose(lse)[:8, :]
    else:
        acc_out[0] = acc[...]
        m_out[0] = m[...]
        l_out[0] = l[...]


def attend(lows, q, fresh, chunks, groups, state, last, patch):
    heads, rows, _ = q.shape
    length = chunks[0].shape[1]
    tile = 256
    first = state is None
    row = pl.BlockSpec((1, tile, HD), lambda h, t: (h, t, 0))
    head = lambda which: (lambda h, t: (which + h, 0, 0))
    inputs, specs = [q], [row]
    if fresh is not None:
        for which in range(2):
            inputs.append(fresh)
            specs.append(pl.BlockSpec((1, fresh.shape[1], HD), head(2 * which)))
    for which in range(2):
        for chunk in chunks:
            inputs.append(chunk)
            specs.append(pl.BlockSpec((1, length, HD), head(2 * which)))
    full = jax.ShapeDtypeStruct((heads, rows, HD), F32)
    if not first:
        inputs += list(state)
        specs += [row] * 3
    if last:
        out_shape = (full, jax.ShapeDtypeStruct((heads, 8, rows), F32))
        out_specs = (row, pl.BlockSpec((1, 8, tile), lambda h, t: (h, 0, t)))
    else:
        out_shape, out_specs = (full,) * 3, (row,) * 3
    tokens = length * len(chunks) + (0 if fresh is None else fresh.shape[1])
    return pl.pallas_call(
        functools.partial(
            attend_kernel, fresh=fresh is not None, groups=groups, first=first, last=last, length=length, patch=patch
        ),
        grid=(heads, rows // tile),
        out_shape=out_shape,
        in_specs=[pl.BlockSpec(memory_space=pltpu.SMEM)] + specs,
        out_specs=out_specs,
        scratch_shapes=[pltpu.VMEM((length * len(chunks), HD), BF)] * 2 + [pltpu.VMEM((tile, HD), F32)] * 3,
        compiler_params=pltpu.CompilerParams(vmem_limit_bytes=40 * 2**20),
        cost_estimate=pl.CostEstimate(
            flops=heads * rows * tokens * HD * 8, bytes_accessed=heads * tokens * HD * 4, transcendentals=heads * rows * tokens
        ),
    )(lows, *inputs)


def body(
    tokens,
    mod_shift,
    mod_scale,
    mod_gate,
    w_query,
    w_key,
    w_value,
    w_out,
    stale_keys,
    stale_values,
    patch_index,
):
    sections = lax.axis_size("section")
    me = lax.axis_index("seq")
    z, y, x = me // PLANE, me // NX % NY, me % NX
    spot = jnp.stack([z, y, x]).astype(jnp.int32)
    rows, width = tokens.shape[1:]
    patch = COUNT * rows
    length = stale_keys.shape[1]
    half = width // NZ

    def kv_chunk(dy, dx, *deps):
        unit = (y + dy) % NY * NX + (x + dx) % NX
        if deps:
            unit = after(unit, *deps)
        parts = []
        for array in (stale_keys, stale_values):
            for plane in (z, 1 - z):
                parts.append(lax.dynamic_slice(array[0], (0, (plane * PLANE + unit) * HD), (length, HD)))
        return jnp.stack(parts)

    inputs = tokens[0].astype(F32)
    meansq = jnp.mean(inputs * inputs, axis=-1, keepdims=True)
    normed = (inputs * lax.rsqrt(meansq + 1e-06) * (1.0 + mod_scale[0]) + mod_shift[0]).astype(BF)
    own = lax.dynamic_slice(normed, (0, z * half), (rows, half))
    sent = lax.dynamic_slice(normed, (0, (1 - z) * half), (rows, half))
    got = moved(sent, dz=1)
    pair = jnp.concatenate((jnp.where(z == 0, own, got), jnp.where(z == 0, got, own)), axis=0)

    stale = {(0, 0): kv_chunk(0, 0)}
    for dy, dx in ((0, 1), (1, 0), (0, 3), (3, 0)):
        stale[dy, dx] = moved(kv_chunk(dy, dx, sent), dy=dy, dx=dx)

    def rows_of(plane):
        return jnp.concatenate(
            [lax.dynamic_slice(w[0], (plane * half, 0), (half, HD)) for w in (w_query, w_key, w_value)], axis=1
        )

    w_got = moved(after(rows_of(1 - z), got), dz=1)
    weights = jnp.concatenate((rows_of(z), w_got), axis=1)

    quarter = half // 2

    def ring(value, axis):
        return jnp.stack([value, moved(value, **{axis: 1}), moved(value, **{axis: 2}), moved(value, **{axis: -1})])

    def spread(block, axis):
        behind = moved(block, **{axis: 1})
        ahead = moved(block, **{axis: -1})
        return [block, behind, ahead, moved(behind[:2], **{axis: 1}), moved(ahead[2:], **{axis: -1})]

    first = ring(pair[:, :quarter], "dy")
    second = ring(pair[:, quarter:], "dx")
    blocks = spread(first, "dx") + spread(second, "dy")
    order = ((0, range(4)), (1, range(4)), (3, range(4)), (2, (0, 1)), (2, (2, 3)))
    pieces = [(0, tuple((j, k) for j in inner)) for k, inner in order]
    pieces += [(quarter, tuple((k, j) for j in inner)) for k, inner in order]

    for dy, dx in ((1, 1), (3, 3), (1, 3)):
        stale[dy, dx] = moved(kv_chunk(dy, dx, pair), dy=dy, dx=dx)
    for dy, dx in ((3, 1), (0, 2), (2, 0), (1, 2), (2, 1), (3, 2), (2, 3), (2, 2)):
        stale[dy, dx] = moved(kv_chunk(dy, dx, first, second), dy=dy, dx=dx)

    q_own, kv_own, sent = project(spot, blocks, pieces, weights, rows)
    got = moved(sent, dz=1)
    q = (q_own + got[1::-1].astype(F32)).astype(BF)
    kv_got = jnp.stack([got[2, patch // 2 :], got[2, : patch // 2], got[3, patch // 2 :], got[3, : patch // 2]])
    fresh = (kv_own + kv_got.astype(F32)).astype(BF)

    wide = width // NX
    w_pair = jnp.concatenate((w_out[0], moved(after(w_out[0], w_got), dz=1)), axis=0)
    w_parts = []
    for k in range(NX):
        part = lax.dynamic_slice(w_pair, (0, (x + k) % NX * wide), (NZ * HD, wide))
        w_parts.append(moved(part, dx=k) if k else part)
    w_columns = jnp.concatenate(w_parts, axis=0)
    tokens_behind = from_behind(tokens[0], "section", 1)
    gate_behind = from_behind(mod_gate, "section", 1)

    offset = patch_index[0] * patch
    keys = list(stale)
    lows = jnp.stack([offset - (z * PLANE + (y - dy) % NY * NX + (x - dx) % NX) * length for dy, dx in keys]).astype(jnp.int32)
    state = attend(lows[:8], q, fresh, [stale[key] for key in keys[:8]], (4, 4), None, False, patch)
    state = attend(lows[8:12], q, None, [stale[key] for key in keys[8:12]], (4,), state, False, patch)
    o, lse = attend(lows[12:], q, None, [stale[key] for key in keys[12:]], (4,), state, True, patch)

    lse = lse[:, 0]
    there = (1 - z) * (patch // 2)
    here = z * (patch // 2)
    o_got = moved(lax.dynamic_slice(o, (0, there, 0), (2, patch // 2, HD)).astype(BF), dz=1)[::-1]
    lse_got = moved(lax.dynamic_slice(lse, (0, there), (2, patch // 2)), dz=1)[::-1]
    o_here = lax.dynamic_slice(o, (0, here, 0), (2, patch // 2, HD))
    lse_here = lax.dynamic_slice(lse, (0, here), (2, patch // 2))
    share = 1.0 / (1.0 + jnp.exp2(lse_got - lse_here))
    share = share[:, :, None]
    attended = (o_here * share + o_got.astype(F32) * (1.0 - share)).astype(BF)
    attended = jnp.concatenate((attended[0], attended[1]), axis=1)

    gathered = jnp.concatenate([attended] + [moved(attended, dx=k) for k in range(1, NX)], axis=1)
    partial = jnp.dot(gathered, w_columns, preferred_element_type=F32).astype(BF)
    band = NX * rows
    total = lax.dynamic_slice(partial, (y * band, 0), (band, wide)).astype(F32)
    for k in range(1, NY):
        part = lax.dynamic_slice(partial, ((y + k) % NY * band, 0), (band, wide))
        total = total + moved(part, dy=k).astype(F32)
    total = total.astype(BF)
    projected = jnp.zeros((rows, width), BF)
    for k in range(NX):
        part = onward(lax.dynamic_slice(total, ((x + k) % NX * rows, 0), (rows, wide)), sections, k)
        projected = lax.dynamic_update_slice(projected, part, (0, (x - k) % NX * wide))
    updated = tokens_behind.astype(F32) + gate_behind * projected.astype(F32)
    return updated.astype(BF)[None]


def solution(mesh):
    placed = (
        P("section", "seq", None),
        P("section", None),
        P("section", None),
        P("section", None),
        P("section", None, "seq"),
        P("section", None, "seq"),
        P("section", None, "seq"),
        P("section", "seq", None),
        P("section", "seq", None),
        P("section", "seq", None),
        P("section"),
    )
    return jax.shard_map(
        body, mesh=mesh, in_specs=placed, out_specs=P("section", "seq", None), check_vma=False
    )
```

```python
import functools

import jax
import jax.numpy as jnp
from jax import lax
from jax.experimental import pallas as pl
from jax.experimental.pallas import tpu as pltpu
from jax.sharding import PartitionSpec as P

HD = 128
NZ, NY, NX = 2, 4, 4
COUNT = NZ * NY * NX
PLANE = NY * NX
LOG2E = 1.4426950408889634
LOWEST = -1e30
BF = jnp.bfloat16
F32 = jnp.float32


def moved(value, dz=0, dy=0, dx=0):
    pairs = []
    for source in range(COUNT):
        z, y, x = source // PLANE, source // NX % NY, source % NX
        target = (z + dz) % NZ * PLANE + (y + dy) % NY * NX + (x + dx) % NX
        pairs.append((source, target))
    return lax.ppermute(value, "seq", pairs)


def onward(value, sections, dx):
    pairs = []
    for section in range(sections):
        for source in range(COUNT):
            target = source // NX * NX + (source % NX + dx) % NX
            pairs.append((section * COUNT + source, (section + 1) % sections * COUNT + target))
    return lax.ppermute(value, ("section", "seq"), pairs)


def from_behind(value, axis, steps):
    count = lax.axis_size(axis)
    pairs = [(source, (source + steps) % count) for source in range(count)]
    return lax.ppermute(value, axis, pairs)


def after(value, *others):
    return lax.optimization_barrier((value,) + others)[0]


def lay_out_kernel(turn, k_ref, v_ref, out_ref):
    for which, ref in enumerate((k_ref, v_ref)):
        for step in range(NZ):
            base = step * PLANE * HD
            for unit in range(PLANE):
                column = base + unit * HD
                out_ref[unit, which * NZ + step] = ref[:, column : column + HD]


def lay_out(turn, keys, values, begin, length):
    rows = 32
    wide = keys.shape[1]
    block = pl.BlockSpec((rows, wide), lambda i: (begin // rows + i, 0))
    return pl.pallas_call(
        lay_out_kernel,
        grid=(length // rows,),
        out_shape=jax.ShapeDtypeStruct((PLANE, 2 * NZ, length, HD), BF),
        in_specs=[pl.BlockSpec(memory_space=pltpu.SMEM), block, block],
        out_specs=pl.BlockSpec((PLANE, 2 * NZ, rows, HD), lambda i: (0, 0, i, 0)),
        compiler_params=pltpu.CompilerParams(vmem_limit_bytes=56 * 2**20),
        cost_estimate=pl.CostEstimate(flops=0, bytes_accessed=PLANE * 4 * NZ * length * HD * 2, transcendentals=0),
    )(turn, keys, values)


def project_kernel(spot, x_hbm, *refs):
    w_hbm, (q_ref, kv_ref, x_ref, w_ref, x_sem, w_sem) = refs[:6], refs[6:]
    tile = x_ref.shape[0] // 2
    x_copies, w_copies = [], []
    for t in range(2):
        some = pl.ds(t * tile, tile)
        x_copies.append(pltpu.make_async_copy(x_hbm.at[some], x_ref.at[some], x_sem.at[t]))
    for at, ref in enumerate(w_hbm):
        w_copies.append(pltpu.make_async_copy(ref, w_ref.at[at // 2, :, pl.ds(at % 2 * HD, HD)], w_sem.at[at]))
    for copy in x_copies[:1] + w_copies[:2] + x_copies[1:] + w_copies[2:]:
        copy.start()
    for kind in range(3):
        for copy in w_copies[2 * kind : 2 * kind + 2]:
            copy.wait()
        for t in range(2):
            if kind == 0:
                x_copies[t].wait()
            some = slice(t * tile, (t + 1) * tile)
            part = jnp.dot(x_ref[some, :], w_ref[kind], preferred_element_type=F32)
            for other in range(NZ):
                head = lax.rem(spot[0] + other, NZ)
                one = part[:, other * HD : (other + 1) * HD]
                if kind == 0:
                    q_ref[head, some, :] = (one * (LOG2E / HD**0.5)).astype(BF)
                else:
                    kv_ref[(kind - 1) * NZ + head, some, :] = one.astype(BF)


def project(spot, normed, weights):
    patch, depth = normed.shape
    vmem = pl.BlockSpec(memory_space=pltpu.VMEM)
    return pl.pallas_call(
        project_kernel,
        out_shape=(jax.ShapeDtypeStruct((NZ, patch, HD), BF), jax.ShapeDtypeStruct((2 * NZ, patch, HD), BF)),
        in_specs=[pl.BlockSpec(memory_space=pltpu.SMEM)] + [pl.BlockSpec(memory_space=pl.ANY)] * 7,
        out_specs=(vmem, vmem),
        scratch_shapes=[
            pltpu.VMEM((patch, depth), BF),
            pltpu.VMEM((3, depth, 2 * HD), BF),
            pltpu.SemaphoreType.DMA((2,)),
            pltpu.SemaphoreType.DMA((6,)),
        ],
        compiler_params=pltpu.CompilerParams(vmem_limit_bytes=58 * 2**20),
        cost_estimate=pl.CostEstimate(
            flops=12 * patch * depth * HD, bytes_accessed=2 * depth * (patch + 6 * HD) + 12 * patch * HD, transcendentals=0
        ),
    )(spot, normed, *weights)


def attend_kernel(spot, here_ref, there_ref, kv_ref, *refs, fresh, first, last, begin, length, patch):
    refs = list(refs)
    if fresh:
        fresh_ref = refs.pop(0)
    if not first:
        acc_in, m_in = refs[:2]
        refs = refs[2:]
    out_refs, (v_wide, acc, m) = refs[:-3], refs[-3:]
    sources, _, share, _ = kv_ref.shape
    size = sources * share
    heads, part, _ = here_ref.shape
    rows = 2 * part
    step = pl.program_id(0)
    sub = 256

    @pl.when(step == 0)
    def _():
        v_wide[:, :, HD:] = jnp.ones((heads, v_wide.shape[1], HD), BF)
        if first:
            m[...] = jnp.full(m.shape, LOWEST, F32)
            acc[...] = jnp.zeros(acc.shape, F32)
        else:
            m[...] = m_in[...]
            acc[...] = acc_in[...]

    def update(keys, count, gone):
        chains = [(head, at) for head in range(heads) for at in range(0, rows, sub)]
        scores = [
            lax.dot_general(
                (here_ref if at < part else there_ref)[head, at % part : at % part + sub],
                keys[head],
                (((1,), (1,)), ((), ())),
                preferred_element_type=F32,
            )
            for head, at in chains
        ]
        for (head, at), s in zip(chains, scores):
            if gone is not None:
                s = jnp.where(gone, LOWEST, s)
            m_old = m[head, at : at + sub]
            m_new = jnp.maximum(m_old, jnp.max(s, axis=1, keepdims=True))
            p = jnp.exp2(s - m_new[:, :1])
            alpha = jnp.exp2(m_old - m_new)
            acc[head, at : at + sub] = jnp.concatenate((alpha, alpha), axis=1) * acc[head, at : at + sub] + jnp.dot(
                p.astype(BF), v_wide[head, :count], preferred_element_type=F32
            )
            m[head, at : at + sub] = m_new

    def low(at):
        return spot[3] - (spot[0] * PLANE + step * sources + at) * length - begin

    touched = jnp.bool_(False)
    for at in range(sources):
        touched = touched | ((low(at) < share) & (low(at) + patch > 0))
    keys = [kv_ref[:, head].reshape(size, HD) for head in range(heads)]
    for head in range(heads):
        v_wide[head, :size, :HD] = kv_ref[:, heads + head].reshape(size, HD)

    @pl.when(touched)
    def _():
        column = lax.broadcasted_iota(jnp.int32, (1, size), 1)
        gone = jnp.zeros((1, size), jnp.int32)
        for at in range(sources):
            start = at * share + jnp.clip(low(at), 0, share)
            end = at * share + jnp.clip(low(at) + patch, 0, share)
            gone = jnp.where((column >= start) & (column < end), 1, gone)
        update(keys, size, gone > 0)

    @pl.when(jnp.logical_not(touched))
    def _():
        update(keys, size, None)

    @pl.when(step == pl.num_programs(0) - 1)
    def _():
        if fresh:
            count = fresh_ref.shape[1]
            for head in range(heads):
                v_wide[head, :count, :HD] = fresh_ref[heads + head]
            update([fresh_ref[head] for head in range(heads)], count, None)
        if last:
            for start, o_ref, lse_ref in ((0, *out_refs[:2]), (part, *out_refs[2:])):
                some = slice(start, start + part)
                for head in range(heads):
                    both = acc[head, some, :]
                    o_ref[head] = (both[:, :HD] / both[:, HD:]).astype(o_ref.dtype)
                    lse_ref[head] = jnp.transpose(m[head, some, :] + jnp.log2(both[:, HD:]))[:8, :]
        else:
            out_refs[0][...] = acc[...]
            out_refs[1][...] = m[...]


def attend(spot, q, stale, fresh, state, last, begin, length, patch, steps):
    heads, rows, _ = q[0].shape
    rows *= 2
    share = stale.shape[2]
    first = state is None
    whole = lambda shape: pl.BlockSpec(shape, lambda g, spot: (0,) * len(shape))
    sources = PLANE // steps
    inputs = [*q, stale]
    specs = [whole(q[0].shape), whole(q[1].shape), pl.BlockSpec((sources, 2 * heads, share, HD), lambda g, spot: (g, 0, 0, 0))]
    count = sources * share
    if fresh is not None:
        inputs.append(fresh)
        specs.append(whole(fresh.shape))
        count = max(count, fresh.shape[1])
    scratch = [pltpu.VMEM((heads, count, 2 * HD), BF), pltpu.VMEM((heads, rows, 2 * HD), F32), pltpu.VMEM((heads, rows, HD), F32)]
    if not first:
        inputs += list(state)
        specs += [whole(part.shape) for part in state]
    shapes = [((heads, rows, 2 * HD), F32), ((heads, rows, HD), F32)]
    if last:
        lse = ((heads, 8, rows // 2), F32)
        shapes = [((heads, rows // 2, HD), F32), lse, ((heads, rows // 2, HD), BF), lse]
    tokens = PLANE * share + (0 if fresh is None else fresh.shape[1])
    return pl.pallas_call(
        functools.partial(
            attend_kernel, fresh=fresh is not None, first=first, last=last, begin=begin, length=length, patch=patch
        ),
        grid_spec=pltpu.PrefetchScalarGridSpec(
            num_scalar_prefetch=1,
            grid=(steps,),
            in_specs=specs,
            out_specs=tuple(whole(shape) for shape, _ in shapes),
            scratch_shapes=scratch,
        ),
        out_shape=tuple(jax.ShapeDtypeStruct(*one) for one in shapes),
        compiler_params=pltpu.CompilerParams(vmem_limit_bytes=56 * 2**20),
        cost_estimate=pl.CostEstimate(
            flops=heads * rows * tokens * HD * 8, bytes_accessed=heads * tokens * HD * 4, transcendentals=heads * rows * tokens
        ),
    )(spot, *inputs)


def body(
    tokens,
    mod_shift,
    mod_scale,
    mod_gate,
    w_query,
    w_key,
    w_value,
    w_out,
    stale_keys,
    stale_values,
    patch_index,
):
    sections = lax.axis_size("section")
    me = lax.axis_index("seq")
    z, y, x = me // PLANE, me // NX % NY, me % NX
    rows, width = tokens.shape[1:]
    patch = COUNT * rows
    length = stale_keys.shape[1]
    spot = jnp.stack([z, y, x, patch_index[0] * patch]).astype(jnp.int32)
    planes = [list(range(plane * PLANE, (plane + 1) * PLANE)) for plane in range(NZ)]

    def stale_laid(begin, share, *deps):
        return lay_out(after(spot[:1], *deps) if deps else spot[:1], stale_keys[0], stale_values[0], begin, share)

    def stale_share(laid, *deps):
        laid = after(laid, *deps) if deps else laid
        return lax.all_to_all(laid, "seq", split_axis=0, concat_axis=0, tiled=True, axis_index_groups=planes)

    weights = []
    for w in (w_query, w_key, w_value):
        weights += [w[0], moved(w[0], dz=1)]

    inputs = tokens[0].astype(F32)
    meansq = jnp.mean(inputs * inputs, axis=-1, keepdims=True)
    normed = (inputs * lax.rsqrt(meansq + 1e-06) * (1.0 + mod_scale[0]) + mod_shift[0]).astype(BF)
    normed = lax.all_gather(normed, "seq", axis=0, tiled=True, axis_index_groups=planes)

    wide = width // NX
    w_slices, w_parts = [], []
    for k in range(NX):
        w_slices.append(lax.dynamic_slice(w_out[0], (0, (x + k) % NX * wide), (HD, wide)))
        w_parts.append(moved(w_slices[k], dx=k) if k else w_slices[k])
    normed, weights, w_parts = lax.optimization_barrier((normed, weights, w_parts))
    w_plane = jnp.concatenate(w_parts, axis=0)

    early = 6 * rows
    stale_first = stale_share(stale_laid(0, early, *w_slices))
    stale_second = stale_share(stale_laid(early, length - early), normed)

    q, fresh = project(spot, normed, weights)
    q = (q, moved(q, dz=1))
    tokens_behind = from_behind(after(tokens[0], q[1]), "section", 1)
    gate_behind = from_behind(after(mod_gate, q[1]), "section", 1)
    w_other = moved(w_plane, dz=1)
    spot, w_other = lax.optimization_barrier((spot, w_other))

    state = attend(spot, q, stale_first, fresh, None, False, 0, length, patch, 4)
    w_columns = jnp.concatenate((jnp.where(z == 0, w_plane, w_other), jnp.where(z == 0, w_other, w_plane)), axis=0)
    o_here, lse_here, o_there, lse_there = attend(spot, q, stale_second, None, state, True, early, length, patch, 4)

    o_got = moved(o_there, dz=1).astype(F32)
    lse_got = moved(lse_there, dz=1)
    part_here = (1.0 / (1.0 + jnp.exp2(lse_got - lse_here)))[:, 0, :, None]
    attended = (o_here * part_here + o_got * (1.0 - part_here)).astype(BF)
    attended = jnp.concatenate((attended[0], attended[1]), axis=1)

    along = [attended] + [moved(attended, dx=k) for k in range(1, NX)]
    gathered = jnp.concatenate([a[:, :HD] for a in along] + [a[:, HD:] for a in along], axis=1)
    partial = jnp.dot(gathered, w_columns, preferred_element_type=F32).astype(BF)
    band = NX * rows
    total = lax.dynamic_slice(partial, (y * band, 0), (band, wide)).astype(F32)
    for k in range(1, NY):
        part = lax.dynamic_slice(partial, ((y + k) % NY * band, 0), (band, wide))
        total = total + moved(part, dy=k).astype(F32)
    total = total.astype(BF)
    projected = jnp.zeros((rows, width), BF)
    for k in range(NX):
        part = onward(lax.dynamic_slice(total, ((x + k) % NX * rows, 0), (rows, wide)), sections, k)
        projected = lax.dynamic_update_slice(projected, part, (0, (x - k) % NX * wide))
    updated = tokens_behind.astype(F32) + gate_behind * projected.astype(F32)
    return updated.astype(BF)[None]


def solution(mesh):
    placed = (
        P("section", "seq", None),
        P("section", None),
        P("section", None),
        P("section", None),
        P("section", None, "seq"),
        P("section", None, "seq"),
        P("section", None, "seq"),
        P("section", "seq", None),
        P("section", "seq", None),
        P("section", "seq", None),
        P("section"),
    )
    return jax.shard_map(
        body, mesh=mesh, in_specs=placed, out_specs=P("section", "seq", None), check_vma=False
    )
```

```python
import functools

import jax
import jax.numpy as jnp
from jax import lax
from jax.experimental import pallas as pl
from jax.experimental.pallas import tpu as pltpu
from jax.sharding import PartitionSpec as P

HD = 128
NZ, NY, NX = 2, 4, 4
COUNT = NZ * NY * NX
PLANE = NY * NX
LOG2E = 1.4426950408889634
LOWEST = -1e30
BF = jnp.bfloat16
F32 = jnp.float32


def moved(value, dz=0, dy=0, dx=0):
    pairs = []
    for source in range(COUNT):
        z, y, x = source // PLANE, source // NX % NY, source % NX
        target = (z + dz) % NZ * PLANE + (y + dy) % NY * NX + (x + dx) % NX
        pairs.append((source, target))
    return lax.ppermute(value, "seq", pairs)


def onward(value, sections, dx):
    pairs = []
    for section in range(sections):
        for source in range(COUNT):
            target = source // NX * NX + (source % NX + dx) % NX
            pairs.append((section * COUNT + source, (section + 1) % sections * COUNT + target))
    return lax.ppermute(value, ("section", "seq"), pairs)


def from_behind(value, axis, steps):
    count = lax.axis_size(axis)
    pairs = [(source, (source + steps) % count) for source in range(count)]
    return lax.ppermute(value, axis, pairs)


def after(value, *others):
    return lax.optimization_barrier((value,) + others)[0]


def lay_out_kernel(turn, k_ref, v_ref, out_ref):
    for which, ref in enumerate((k_ref, v_ref)):
        for step in range(NZ):
            base = step * PLANE * HD
            for unit in range(PLANE):
                column = base + unit * HD
                out_ref[unit, which * NZ + step] = ref[:, column : column + HD]


def lay_out(turn, keys, values, begin, length):
    rows = 32
    wide = keys.shape[1]
    block = pl.BlockSpec((rows, wide), lambda i: (begin // rows + i, 0))
    return pl.pallas_call(
        lay_out_kernel,
        grid=(length // rows,),
        out_shape=jax.ShapeDtypeStruct((PLANE, 2 * NZ, length, HD), BF),
        in_specs=[pl.BlockSpec(memory_space=pltpu.SMEM), block, block],
        out_specs=pl.BlockSpec((PLANE, 2 * NZ, rows, HD), lambda i: (0, 0, i, 0)),
        compiler_params=pltpu.CompilerParams(vmem_limit_bytes=56 * 2**20),
        cost_estimate=pl.CostEstimate(flops=0, bytes_accessed=PLANE * 4 * NZ * length * HD * 2, transcendentals=0),
    )(turn, keys, values)


def project_kernel(spot, x_hbm, *refs, scale):
    kinds = (len(refs) - 5) // 2
    w_hbm, (out_ref, x_ref, w_ref, x_sem, w_sem) = refs[: 2 * kinds], refs[2 * kinds :]
    tile = x_ref.shape[0] // 2
    x_copies, w_copies = [], []
    for t in range(2):
        some = pl.ds(t * tile, tile)
        x_copies.append(pltpu.make_async_copy(x_hbm.at[some], x_ref.at[some], x_sem.at[t]))
    for at, ref in enumerate(w_hbm):
        w_copies.append(pltpu.make_async_copy(ref, w_ref.at[at // 2, :, pl.ds(at % 2 * HD, HD)], w_sem.at[at]))
    for copy in x_copies[:1] + w_copies[:2] + x_copies[1:] + w_copies[2:]:
        copy.start()
    for kind in range(kinds):
        for copy in w_copies[2 * kind : 2 * kind + 2]:
            copy.wait()
        for t in range(2):
            if kind == 0:
                x_copies[t].wait()
            some = slice(t * tile, (t + 1) * tile)
            part = jnp.dot(x_ref[some, :], w_ref[kind], preferred_element_type=F32)
            for other in range(NZ):
                one = part[:, other * HD : (other + 1) * HD]
                out_ref[kind * NZ + lax.rem(spot[0] + other, NZ), some, :] = (one * scale).astype(BF)


def project(spot, normed, weights, scale):
    kinds = len(weights) // 2
    patch, depth = normed.shape
    return pl.pallas_call(
        functools.partial(project_kernel, scale=scale),
        out_shape=jax.ShapeDtypeStruct((kinds * NZ, patch, HD), BF),
        in_specs=[pl.BlockSpec(memory_space=pltpu.SMEM)] + [pl.BlockSpec(memory_space=pl.ANY)] * (1 + 2 * kinds),
        out_specs=pl.BlockSpec(memory_space=pltpu.VMEM),
        scratch_shapes=[
            pltpu.VMEM((patch, depth), BF),
            pltpu.VMEM((kinds, depth, 2 * HD), BF),
            pltpu.SemaphoreType.DMA((2,)),
            pltpu.SemaphoreType.DMA((2 * kinds,)),
        ],
        compiler_params=pltpu.CompilerParams(vmem_limit_bytes=58 * 2**20),
        cost_estimate=pl.CostEstimate(
            flops=4 * kinds * patch * depth * HD, bytes_accessed=2 * depth * (patch + 2 * kinds * HD) + 4 * patch * HD * kinds, transcendentals=0
        ),
    )(spot, normed, *weights)


def attend_kernel(spot, here_ref, there_ref, kv_ref, *refs, fresh, first, last, begin, length, patch):
    refs = list(refs)
    if fresh:
        fresh_ref = refs.pop(0)
    if not first:
        acc_in, m_in = refs[:2]
        refs = refs[2:]
    out_refs, (v_wide, acc, m) = refs[:-3], refs[-3:]
    sources, _, share, _ = kv_ref.shape
    size = sources * share
    heads, part, _ = here_ref.shape
    rows = 2 * part
    step = pl.program_id(0)
    sub = 256

    @pl.when(step == 0)
    def _():
        v_wide[:, :, HD:] = jnp.ones((heads, v_wide.shape[1], HD), BF)
        if first:
            m[...] = jnp.full(m.shape, LOWEST, F32)
            acc[...] = jnp.zeros(acc.shape, F32)
        else:
            m[...] = m_in[...]
            acc[...] = acc_in[...]

    def update(keys, count, gone):
        chains = [(head, at) for head in range(heads) for at in range(0, rows, sub)]
        scores = [
            lax.dot_general(
                (here_ref if at < part else there_ref)[head, at % part : at % part + sub],
                keys[head],
                (((1,), (1,)), ((), ())),
                preferred_element_type=F32,
            )
            for head, at in chains
        ]
        for (head, at), s in zip(chains, scores):
            if gone is not None:
                s = jnp.where(gone, LOWEST, s)
            m_old = m[head, at : at + sub]
            m_new = jnp.maximum(m_old, jnp.max(s, axis=1, keepdims=True))
            p = jnp.exp2(s - m_new[:, :1])
            alpha = jnp.exp2(m_old - m_new)
            acc[head, at : at + sub] = jnp.concatenate((alpha, alpha), axis=1) * acc[head, at : at + sub] + jnp.dot(
                p.astype(BF), v_wide[head, :count], preferred_element_type=F32
            )
            m[head, at : at + sub] = m_new

    def low(at):
        return spot[3] - (spot[0] * PLANE + step * sources + at) * length - begin

    touched = jnp.bool_(False)
    for at in range(sources):
        touched = touched | ((low(at) < share) & (low(at) + patch > 0))
    keys = [kv_ref[:, head].reshape(size, HD) for head in range(heads)]
    for head in range(heads):
        v_wide[head, :size, :HD] = kv_ref[:, heads + head].reshape(size, HD)

    @pl.when(touched)
    def _():
        column = lax.broadcasted_iota(jnp.int32, (1, size), 1)
        gone = jnp.zeros((1, size), jnp.int32)
        for at in range(sources):
            start = at * share + jnp.clip(low(at), 0, share)
            end = at * share + jnp.clip(low(at) + patch, 0, share)
            gone = jnp.where((column >= start) & (column < end), 1, gone)
        update(keys, size, gone > 0)

    @pl.when(jnp.logical_not(touched))
    def _():
        update(keys, size, None)

    @pl.when(step == pl.num_programs(0) - 1)
    def _():
        if fresh:
            count = fresh_ref.shape[1]
            for head in range(heads):
                v_wide[head, :count, :HD] = fresh_ref[heads + head]
            update([fresh_ref[head] for head in range(heads)], count, None)
        if last:
            for start, o_ref, lse_ref in ((0, *out_refs[:2]), (part, *out_refs[2:])):
                some = slice(start, start + part)
                for head in range(heads):
                    both = acc[head, some, :]
                    o_ref[head] = (both[:, :HD] / both[:, HD:]).astype(o_ref.dtype)
                    lse_ref[head] = jnp.transpose(m[head, some, :] + jnp.log2(both[:, HD:]))[:8, :]
        else:
            out_refs[0][...] = acc[...]
            out_refs[1][...] = m[...]


def attend(spot, q, stale, fresh, state, last, begin, length, patch, steps):
    heads, rows, _ = q[0].shape
    rows *= 2
    share = stale.shape[2]
    first = state is None
    whole = lambda shape: pl.BlockSpec(shape, lambda g, spot: (0,) * len(shape))
    sources = PLANE // steps
    inputs = [*q, stale]
    specs = [whole(q[0].shape), whole(q[1].shape), pl.BlockSpec((sources, 2 * heads, share, HD), lambda g, spot: (g, 0, 0, 0))]
    count = sources * share
    if fresh is not None:
        inputs.append(fresh)
        specs.append(whole(fresh.shape))
        count = max(count, fresh.shape[1])
    scratch = [pltpu.VMEM((heads, count, 2 * HD), BF), pltpu.VMEM((heads, rows, 2 * HD), F32), pltpu.VMEM((heads, rows, HD), F32)]
    if not first:
        inputs += list(state)
        specs += [whole(part.shape) for part in state]
    shapes = [((heads, rows, 2 * HD), F32), ((heads, rows, HD), F32)]
    if last:
        lse = ((heads, 8, rows // 2), F32)
        shapes = [((heads, rows // 2, HD), F32), lse, ((heads, rows // 2, HD), BF), lse]
    tokens = PLANE * share + (0 if fresh is None else fresh.shape[1])
    return pl.pallas_call(
        functools.partial(
            attend_kernel, fresh=fresh is not None, first=first, last=last, begin=begin, length=length, patch=patch
        ),
        grid_spec=pltpu.PrefetchScalarGridSpec(
            num_scalar_prefetch=1,
            grid=(steps,),
            in_specs=specs,
            out_specs=tuple(whole(shape) for shape, _ in shapes),
            scratch_shapes=scratch,
        ),
        out_shape=tuple(jax.ShapeDtypeStruct(*one) for one in shapes),
        compiler_params=pltpu.CompilerParams(vmem_limit_bytes=56 * 2**20),
        cost_estimate=pl.CostEstimate(
            flops=heads * rows * tokens * HD * 8, bytes_accessed=heads * tokens * HD * 4, transcendentals=heads * rows * tokens
        ),
    )(spot, *inputs)


def body(
    tokens,
    mod_shift,
    mod_scale,
    mod_gate,
    w_query,
    w_key,
    w_value,
    w_out,
    stale_keys,
    stale_values,
    patch_index,
):
    sections = lax.axis_size("section")
    me = lax.axis_index("seq")
    z, y, x = me // PLANE, me // NX % NY, me % NX
    rows, width = tokens.shape[1:]
    patch = COUNT * rows
    length = stale_keys.shape[1]
    spot = jnp.stack([z, y, x, patch_index[0] * patch]).astype(jnp.int32)
    planes = [list(range(plane * PLANE, (plane + 1) * PLANE)) for plane in range(NZ)]

    def stale_laid(begin, share, *deps):
        return lay_out(after(spot[:1], *deps) if deps else spot[:1], stale_keys[0], stale_values[0], begin, share)

    def stale_share(laid, *deps):
        laid = after(laid, *deps) if deps else laid
        return lax.all_to_all(laid, "seq", split_axis=0, concat_axis=0, tiled=True, axis_index_groups=planes)

    weights = []
    for w in (w_query, w_key, w_value):
        weights += [w[0], moved(w[0], dz=1)]

    inputs = tokens[0].astype(F32)
    meansq = jnp.mean(inputs * inputs, axis=-1, keepdims=True)
    normed = (inputs * lax.rsqrt(meansq + 1e-06) * (1.0 + mod_scale[0]) + mod_shift[0]).astype(BF)
    normed = lax.all_gather(normed, "seq", axis=0, tiled=True, axis_index_groups=planes)

    wide = width // NX
    w_slices, w_parts = [], []
    for k in range(NX):
        w_slices.append(lax.dynamic_slice(w_out[0], (0, (x + k) % NX * wide), (HD, wide)))
        w_parts.append(moved(w_slices[k], dx=k) if k else w_slices[k])
    normed, weights, w_parts = lax.optimization_barrier((normed, weights, w_parts))
    w_plane = jnp.concatenate(w_parts, axis=0)

    early = 6 * rows
    stale_first = stale_share(stale_laid(0, early, *w_slices))
    stale_second = stale_share(stale_laid(early, length - early), normed)

    q = project(spot, normed, weights[:2], LOG2E / HD**0.5)
    q_there = moved(q, dz=1)
    spot, q = lax.optimization_barrier((spot, q))
    fresh = project(spot, normed, weights[2:], 1.0)
    w_other = moved(after(w_plane, q_there), dz=1)
    tokens_behind = from_behind(after(tokens[0], q_there), "section", 1)
    gate_behind = from_behind(after(mod_gate, q_there), "section", 1)

    q = (q, q_there)
    state = attend(spot, q, stale_first, None, None, False, 0, length, patch, 4)
    fresh, w_other = lax.optimization_barrier((fresh, w_other))
    w_columns = jnp.concatenate((jnp.where(z == 0, w_plane, w_other), jnp.where(z == 0, w_other, w_plane)), axis=0)
    o_here, lse_here, o_there, lse_there = attend(spot, q, stale_second, fresh, state, True, early, length, patch, 4)

    o_got = moved(o_there, dz=1).astype(F32)
    lse_got = moved(lse_there, dz=1)
    part_here = (1.0 / (1.0 + jnp.exp2(lse_got - lse_here)))[:, 0, :, None]
    attended = (o_here * part_here + o_got * (1.0 - part_here)).astype(BF)
    attended = jnp.concatenate((attended[0], attended[1]), axis=1)

    along = [attended] + [moved(attended, dx=k) for k in range(1, NX)]
    gathered = jnp.concatenate([a[:, :HD] for a in along] + [a[:, HD:] for a in along], axis=1)
    partial = jnp.dot(gathered, w_columns, preferred_element_type=F32).astype(BF)
    band = NX * rows
    total = lax.dynamic_slice(partial, (y * band, 0), (band, wide)).astype(F32)
    for k in range(1, NY):
        part = lax.dynamic_slice(partial, ((y + k) % NY * band, 0), (band, wide))
        total = total + moved(part, dy=k).astype(F32)
    total = total.astype(BF)
    projected = jnp.zeros((rows, width), BF)
    for k in range(NX):
        part = onward(lax.dynamic_slice(total, ((x + k) % NX * rows, 0), (rows, wide)), sections, k)
        projected = lax.dynamic_update_slice(projected, part, (0, (x - k) % NX * wide))
    updated = tokens_behind.astype(F32) + gate_behind * projected.astype(F32)
    return updated.astype(BF)[None]


def solution(mesh):
    placed = (
        P("section", "seq", None),
        P("section", None),
        P("section", None),
        P("section", None),
        P("section", None, "seq"),
        P("section", None, "seq"),
        P("section", None, "seq"),
        P("section", "seq", None),
        P("section", "seq", None),
        P("section", "seq", None),
        P("section"),
    )
    return jax.shard_map(
        body, mesh=mesh, in_specs=placed, out_specs=P("section", "seq", None), check_vma=False
    )
```

```python
import functools

import jax
import jax.numpy as jnp
from jax import lax
from jax.experimental import pallas as pl
from jax.experimental.pallas import tpu as pltpu
from jax.sharding import PartitionSpec as P

HD = 128
NZ, NY, NX = 2, 4, 4
COUNT = NZ * NY * NX
PLANE = NY * NX
LOG2E = 1.4426950408889634
LOWEST = -1e30
BF = jnp.bfloat16
F32 = jnp.float32


def moved(value, dz=0, dy=0, dx=0):
    pairs = []
    for source in range(COUNT):
        z, y, x = source // PLANE, source // NX % NY, source % NX
        target = (z + dz) % NZ * PLANE + (y + dy) % NY * NX + (x + dx) % NX
        pairs.append((source, target))
    return lax.ppermute(value, "seq", pairs)


def onward(value, sections, dx):
    pairs = []
    for section in range(sections):
        for source in range(COUNT):
            target = source // NX * NX + (source % NX + dx) % NX
            pairs.append((section * COUNT + source, (section + 1) % sections * COUNT + target))
    return lax.ppermute(value, ("section", "seq"), pairs)


def from_behind(value, axis, steps):
    count = lax.axis_size(axis)
    pairs = [(source, (source + steps) % count) for source in range(count)]
    return lax.ppermute(value, axis, pairs)


def after(value, *others):
    return lax.optimization_barrier((value,) + others)[0]


def lay_out_kernel(turn, k_ref, v_ref, out_ref):
    for which, ref in enumerate((k_ref, v_ref)):
        for step in range(NZ):
            base = step * PLANE * HD
            for unit in range(PLANE):
                column = base + unit * HD
                out_ref[unit, which * NZ + step] = ref[:, column : column + HD]


def lay_out(turn, keys, values, begin, length):
    rows = 32
    wide = keys.shape[1]
    block = pl.BlockSpec((rows, wide), lambda i: (begin // rows + i, 0))
    return pl.pallas_call(
        lay_out_kernel,
        grid=(length // rows,),
        out_shape=jax.ShapeDtypeStruct((PLANE, 2 * NZ, length, HD), BF),
        in_specs=[pl.BlockSpec(memory_space=pltpu.SMEM), block, block],
        out_specs=pl.BlockSpec((PLANE, 2 * NZ, rows, HD), lambda i: (0, 0, i, 0)),
        compiler_params=pltpu.CompilerParams(vmem_limit_bytes=56 * 2**20),
        cost_estimate=pl.CostEstimate(flops=0, bytes_accessed=PLANE * 4 * NZ * length * HD * 2, transcendentals=0),
    )(turn, keys, values)


def project_kernel(spot, x_hbm, *refs, scale):
    kinds = (len(refs) - 5) // 2
    w_hbm, (out_ref, x_ref, w_ref, x_sem, w_sem) = refs[: 2 * kinds], refs[2 * kinds :]
    tile = x_ref.shape[0] // 2
    x_copies, w_copies = [], []
    for t in range(2):
        some = pl.ds(t * tile, tile)
        x_copies.append(pltpu.make_async_copy(x_hbm.at[some], x_ref.at[some], x_sem.at[t]))
    for at, ref in enumerate(w_hbm):
        w_copies.append(pltpu.make_async_copy(ref, w_ref.at[at // 2, :, pl.ds(at % 2 * HD, HD)], w_sem.at[at]))
    for copy in x_copies[:1] + w_copies[:2] + x_copies[1:] + w_copies[2:]:
        copy.start()
    for kind in range(kinds):
        for copy in w_copies[2 * kind : 2 * kind + 2]:
            copy.wait()
        for t in range(2):
            if kind == 0:
                x_copies[t].wait()
            some = slice(t * tile, (t + 1) * tile)
            part = jnp.dot(x_ref[some, :], w_ref[kind], preferred_element_type=F32)
            for other in range(NZ):
                one = part[:, other * HD : (other + 1) * HD]
                out_ref[kind * NZ + lax.rem(spot[0] + other, NZ), some, :] = (one * scale).astype(BF)


def project(spot, normed, weights, scale):
    kinds = len(weights) // 2
    patch, depth = normed.shape
    return pl.pallas_call(
        functools.partial(project_kernel, scale=scale),
        out_shape=jax.ShapeDtypeStruct((kinds * NZ, patch, HD), BF),
        in_specs=[pl.BlockSpec(memory_space=pltpu.SMEM)] + [pl.BlockSpec(memory_space=pl.ANY)] * (1 + 2 * kinds),
        out_specs=pl.BlockSpec(memory_space=pltpu.VMEM),
        scratch_shapes=[
            pltpu.VMEM((patch, depth), BF),
            pltpu.VMEM((kinds, depth, 2 * HD), BF),
            pltpu.SemaphoreType.DMA((2,)),
            pltpu.SemaphoreType.DMA((2 * kinds,)),
        ],
        compiler_params=pltpu.CompilerParams(vmem_limit_bytes=58 * 2**20),
        cost_estimate=pl.CostEstimate(
            flops=4 * kinds * patch * depth * HD, bytes_accessed=2 * depth * (patch + 2 * kinds * HD) + 4 * patch * HD * kinds, transcendentals=0
        ),
    )(spot, normed, *weights)


def attend_kernel(spot, here_ref, there_ref, kv_ref, *refs, fresh, first, last, begin, length, patch):
    refs = list(refs)
    if fresh:
        fresh_ref = refs.pop(0)
    if not first:
        acc_in, m_in = refs[:2]
        refs = refs[2:]
    out_refs, (v_wide, acc, m) = refs[:-3], refs[-3:]
    sources, _, share, _ = kv_ref.shape
    size = sources * share
    heads, part, _ = here_ref.shape
    rows = 2 * part
    step = pl.program_id(0)
    sub = 256

    @pl.when(step == 0)
    def _():
        v_wide[:, :, HD:] = jnp.ones((heads, v_wide.shape[1], HD), BF)
        if first:
            m[...] = jnp.full(m.shape, LOWEST, F32)
            acc[...] = jnp.zeros(acc.shape, F32)
        else:
            m[...] = m_in[...]
            acc[...] = acc_in[...]

    def update(keys, count, gone):
        chains = [(head, at) for head in range(heads) for at in range(0, rows, sub)]
        scores = [
            lax.dot_general(
                (here_ref if at < part else there_ref)[head, at % part : at % part + sub],
                keys[head],
                (((1,), (1,)), ((), ())),
                preferred_element_type=F32,
            )
            for head, at in chains
        ]
        for (head, at), s in zip(chains, scores):
            if gone is not None:
                s = jnp.where(gone, LOWEST, s)
            m_old = m[head, at : at + sub]
            m_new = jnp.maximum(m_old, jnp.max(s, axis=1, keepdims=True))
            p = jnp.exp2(s - m_new[:, :1])
            alpha = jnp.exp2(m_old - m_new)
            acc[head, at : at + sub] = jnp.concatenate((alpha, alpha), axis=1) * acc[head, at : at + sub] + jnp.dot(
                p.astype(BF), v_wide[head, :count], preferred_element_type=F32
            )
            m[head, at : at + sub] = m_new

    def low(at):
        return spot[3] - (spot[0] * PLANE + step * sources + at) * length - begin

    touched = jnp.bool_(False)
    for at in range(sources):
        touched = touched | ((low(at) < share) & (low(at) + patch > 0))
    keys = [kv_ref[:, head].reshape(size, HD) for head in range(heads)]
    for head in range(heads):
        v_wide[head, :size, :HD] = kv_ref[:, heads + head].reshape(size, HD)

    @pl.when(touched)
    def _():
        column = lax.broadcasted_iota(jnp.int32, (1, size), 1)
        gone = jnp.zeros((1, size), jnp.int32)
        for at in range(sources):
            start = at * share + jnp.clip(low(at), 0, share)
            end = at * share + jnp.clip(low(at) + patch, 0, share)
            gone = jnp.where((column >= start) & (column < end), 1, gone)
        update(keys, size, gone > 0)

    @pl.when(jnp.logical_not(touched))
    def _():
        update(keys, size, None)

    @pl.when(step == pl.num_programs(0) - 1)
    def _():
        if fresh:
            count = fresh_ref.shape[1]
            for head in range(heads):
                v_wide[head, :count, :HD] = fresh_ref[heads + head]
            update([fresh_ref[head] for head in range(heads)], count, None)
        if last:
            for start, o_ref, lse_ref in ((0, *out_refs[:2]), (part, *out_refs[2:])):
                some = slice(start, start + part)
                for head in range(heads):
                    both = acc[head, some, :]
                    o_ref[head] = (both[:, :HD] / both[:, HD:]).astype(o_ref.dtype)
                    lse_ref[head] = jnp.transpose(m[head, some, :] + jnp.log2(both[:, HD:]))[:8, :]
        else:
            out_refs[0][...] = acc[...]
            out_refs[1][...] = m[...]


def attend(spot, q, stale, fresh, state, last, begin, length, patch, steps):
    heads, rows, _ = q[0].shape
    rows *= 2
    share = stale.shape[2]
    first = state is None
    whole = lambda shape: pl.BlockSpec(shape, lambda g, spot: (0,) * len(shape))
    sources = PLANE // steps
    inputs = [*q, stale]
    specs = [whole(q[0].shape), whole(q[1].shape), pl.BlockSpec((sources, 2 * heads, share, HD), lambda g, spot: (g, 0, 0, 0))]
    count = sources * share
    if fresh is not None:
        inputs.append(fresh)
        specs.append(whole(fresh.shape))
        count = max(count, fresh.shape[1])
    scratch = [pltpu.VMEM((heads, count, 2 * HD), BF), pltpu.VMEM((heads, rows, 2 * HD), F32), pltpu.VMEM((heads, rows, HD), F32)]
    if not first:
        inputs += list(state)
        specs += [whole(part.shape) for part in state]
    shapes = [((heads, rows, 2 * HD), F32), ((heads, rows, HD), F32)]
    if last:
        lse = ((heads, 8, rows // 2), F32)
        shapes = [((heads, rows // 2, HD), F32), lse, ((heads, rows // 2, HD), BF), lse]
    tokens = PLANE * share + (0 if fresh is None else fresh.shape[1])
    return pl.pallas_call(
        functools.partial(
            attend_kernel, fresh=fresh is not None, first=first, last=last, begin=begin, length=length, patch=patch
        ),
        grid_spec=pltpu.PrefetchScalarGridSpec(
            num_scalar_prefetch=1,
            grid=(steps,),
            in_specs=specs,
            out_specs=tuple(whole(shape) for shape, _ in shapes),
            scratch_shapes=scratch,
        ),
        out_shape=tuple(jax.ShapeDtypeStruct(*one) for one in shapes),
        compiler_params=pltpu.CompilerParams(vmem_limit_bytes=56 * 2**20),
        cost_estimate=pl.CostEstimate(
            flops=heads * rows * tokens * HD * 8, bytes_accessed=heads * tokens * HD * 4, transcendentals=heads * rows * tokens
        ),
    )(spot, *inputs)


def body(
    tokens,
    mod_shift,
    mod_scale,
    mod_gate,
    w_query,
    w_key,
    w_value,
    w_out,
    stale_keys,
    stale_values,
    patch_index,
):
    sections = lax.axis_size("section")
    me = lax.axis_index("seq")
    z, y, x = me // PLANE, me // NX % NY, me % NX
    rows, width = tokens.shape[1:]
    patch = COUNT * rows
    length = stale_keys.shape[1]
    spot = jnp.stack([z, y, x, patch_index[0] * patch]).astype(jnp.int32)
    planes = [list(range(plane * PLANE, (plane + 1) * PLANE)) for plane in range(NZ)]

    def stale_laid(begin, share, *deps):
        return lay_out(after(spot[:1], *deps) if deps else spot[:1], stale_keys[0], stale_values[0], begin, share)

    def stale_share(laid, *deps):
        laid = after(laid, *deps) if deps else laid
        return lax.all_to_all(laid, "seq", split_axis=0, concat_axis=0, tiled=True, axis_index_groups=planes)

    weights = []
    for w in (w_query, w_key, w_value):
        weights += [w[0], moved(w[0], dz=1)]

    inputs = tokens[0].astype(F32)
    meansq = jnp.mean(inputs * inputs, axis=-1, keepdims=True)
    normed = (inputs * lax.rsqrt(meansq + 1e-06) * (1.0 + mod_scale[0]) + mod_shift[0]).astype(BF)
    normed = lax.all_gather(normed, "seq", axis=0, tiled=True, axis_index_groups=planes)

    wide = width // NX
    w_slices, w_parts = [], []
    for k in range(NX):
        w_slices.append(lax.dynamic_slice(w_out[0], (0, (x + k) % NX * wide), (HD, wide)))
        w_parts.append(moved(w_slices[k], dx=k) if k else w_slices[k])
    q = project(spot, normed, weights[:2], LOG2E / HD**0.5)
    q_there = moved(q, dz=1)
    normed, weights, w_parts = lax.optimization_barrier((normed, weights, w_parts))
    w_plane = jnp.concatenate(w_parts, axis=0)

    early = 8 * rows
    stale_first = stale_share(stale_laid(0, early, *w_slices))
    stale_second = stale_share(stale_laid(early, length - early), normed)

    spot, q = lax.optimization_barrier((spot, q))
    fresh = project(spot, normed, weights[2:], 1.0)
    w_other = moved(after(w_plane, q_there), dz=1)
    tokens_behind = from_behind(after(tokens[0], q_there), "section", 1)
    gate_behind = from_behind(after(mod_gate, q_there), "section", 1)

    q = (q, q_there)
    state = attend(spot, q, stale_first, None, None, False, 0, length, patch, 4)
    fresh, w_other = lax.optimization_barrier((fresh, w_other))
    w_columns = jnp.concatenate((jnp.where(z == 0, w_plane, w_other), jnp.where(z == 0, w_other, w_plane)), axis=0)
    o_here, lse_here, o_there, lse_there = attend(spot, q, stale_second, fresh, state, True, early, length, patch, 4)

    o_got = moved(o_there, dz=1).astype(F32)
    lse_got = moved(lse_there, dz=1)
    part_here = (1.0 / (1.0 + jnp.exp2(lse_got - lse_here)))[:, 0, :, None]
    attended = (o_here * part_here + o_got * (1.0 - part_here)).astype(BF)
    attended = jnp.concatenate((attended[0], attended[1]), axis=1)

    along = [attended] + [moved(attended, dx=k) for k in range(1, NX)]
    gathered = jnp.concatenate([a[:, :HD] for a in along] + [a[:, HD:] for a in along], axis=1)
    partial = jnp.dot(gathered, w_columns, preferred_element_type=F32).astype(BF)
    band = NX * rows
    total = lax.dynamic_slice(partial, (y * band, 0), (band, wide)).astype(F32)
    for k in range(1, NY):
        part = lax.dynamic_slice(partial, ((y + k) % NY * band, 0), (band, wide))
        total = total + moved(part, dy=k).astype(F32)
    total = total.astype(BF)
    projected = jnp.zeros((rows, width), BF)
    for k in range(NX):
        part = onward(lax.dynamic_slice(total, ((x + k) % NX * rows, 0), (rows, wide)), sections, k)
        projected = lax.dynamic_update_slice(projected, part, (0, (x - k) % NX * wide))
    updated = tokens_behind.astype(F32) + gate_behind * projected.astype(F32)
    return updated.astype(BF)[None]


def solution(mesh):
    placed = (
        P("section", "seq", None),
        P("section", None),
        P("section", None),
        P("section", None),
        P("section", None, "seq"),
        P("section", None, "seq"),
        P("section", None, "seq"),
        P("section", "seq", None),
        P("section", "seq", None),
        P("section", "seq", None),
        P("section"),
    )
    return jax.shard_map(
        body, mesh=mesh, in_specs=placed, out_specs=P("section", "seq", None), check_vma=False
    )
```

```python
import functools

import jax
import jax.numpy as jnp
from jax import lax
from jax.experimental import pallas as pl
from jax.experimental.pallas import tpu as pltpu
from jax.sharding import PartitionSpec as P

HD = 128
NZ, NY, NX = 2, 4, 4
COUNT = NZ * NY * NX
PLANE = NY * NX
LOG2E = 1.4426950408889634
LOWEST = -1e30
BF = jnp.bfloat16
F32 = jnp.float32


def moved(value, dz=0, dy=0, dx=0):
    pairs = []
    for source in range(COUNT):
        z, y, x = source // PLANE, source // NX % NY, source % NX
        target = (z + dz) % NZ * PLANE + (y + dy) % NY * NX + (x + dx) % NX
        pairs.append((source, target))
    return lax.ppermute(value, "seq", pairs)


def onward(value, sections, dx):
    pairs = []
    for section in range(sections):
        for source in range(COUNT):
            target = source // NX * NX + (source % NX + dx) % NX
            pairs.append((section * COUNT + source, (section + 1) % sections * COUNT + target))
    return lax.ppermute(value, ("section", "seq"), pairs)


def from_behind(value, axis, steps):
    count = lax.axis_size(axis)
    pairs = [(source, (source + steps) % count) for source in range(count)]
    return lax.ppermute(value, axis, pairs)


def after(value, *others):
    return lax.optimization_barrier((value,) + others)[0]


def lay_out_kernel(turn, k_ref, v_ref, out_ref):
    for which, ref in enumerate((k_ref, v_ref)):
        for step in range(NZ):
            base = step * PLANE * HD
            for unit in range(PLANE):
                column = base + unit * HD
                out_ref[unit, which * NZ + step] = ref[:, column : column + HD]


def lay_out(turn, keys, values, begin, length):
    rows = 32
    wide = keys.shape[1]
    block = pl.BlockSpec((rows, wide), lambda i: (begin // rows + i, 0))
    return pl.pallas_call(
        lay_out_kernel,
        grid=(length // rows,),
        out_shape=jax.ShapeDtypeStruct((PLANE, 2 * NZ, length, HD), BF),
        in_specs=[pl.BlockSpec(memory_space=pltpu.SMEM), block, block],
        out_specs=pl.BlockSpec((PLANE, 2 * NZ, rows, HD), lambda i: (0, 0, i, 0)),
        compiler_params=pltpu.CompilerParams(vmem_limit_bytes=56 * 2**20),
        cost_estimate=pl.CostEstimate(flops=0, bytes_accessed=PLANE * 4 * NZ * length * HD * 2, transcendentals=0),
    )(turn, keys, values)


def project_kernel(spot, x_hbm, *refs, scale):
    kinds = (len(refs) - 5) // 2
    w_hbm, (out_ref, x_ref, w_ref, x_sem, w_sem) = refs[: 2 * kinds], refs[2 * kinds :]
    tile = x_ref.shape[0] // 2
    x_copies, w_copies = [], []
    for t in range(2):
        some = pl.ds(t * tile, tile)
        x_copies.append(pltpu.make_async_copy(x_hbm.at[some], x_ref.at[some], x_sem.at[t]))
    for at, ref in enumerate(w_hbm):
        w_copies.append(pltpu.make_async_copy(ref, w_ref.at[at // 2, :, pl.ds(at % 2 * HD, HD)], w_sem.at[at]))
    for copy in x_copies[:1] + w_copies[:2] + x_copies[1:] + w_copies[2:]:
        copy.start()
    for kind in range(kinds):
        for copy in w_copies[2 * kind : 2 * kind + 2]:
            copy.wait()
        for t in range(2):
            if kind == 0:
                x_copies[t].wait()
            some = slice(t * tile, (t + 1) * tile)
            part = jnp.dot(x_ref[some, :], w_ref[kind], preferred_element_type=F32)
            for other in range(NZ):
                one = part[:, other * HD : (other + 1) * HD]
                out_ref[kind * NZ + lax.rem(spot[0] + other, NZ), some, :] = (one * scale).astype(BF)


def project(spot, normed, weights, scale):
    kinds = len(weights) // 2
    patch, depth = normed.shape
    return pl.pallas_call(
        functools.partial(project_kernel, scale=scale),
        out_shape=jax.ShapeDtypeStruct((kinds * NZ, patch, HD), BF),
        in_specs=[pl.BlockSpec(memory_space=pltpu.SMEM)] + [pl.BlockSpec(memory_space=pl.ANY)] * (1 + 2 * kinds),
        out_specs=pl.BlockSpec(memory_space=pltpu.VMEM),
        scratch_shapes=[
            pltpu.VMEM((patch, depth), BF),
            pltpu.VMEM((kinds, depth, 2 * HD), BF),
            pltpu.SemaphoreType.DMA((2,)),
            pltpu.SemaphoreType.DMA((2 * kinds,)),
        ],
        compiler_params=pltpu.CompilerParams(vmem_limit_bytes=58 * 2**20),
        cost_estimate=pl.CostEstimate(
            flops=4 * kinds * patch * depth * HD, bytes_accessed=2 * depth * (patch + 2 * kinds * HD) + 4 * patch * HD * kinds, transcendentals=0
        ),
    )(spot, normed, *weights)


def attend_kernel(spot, here_ref, there_ref, kv_ref, *refs, fresh, first, last, begin, length, patch):
    refs = list(refs)
    if fresh:
        fresh_ref = refs.pop(0)
    if not first:
        acc_in, m_in = refs[:2]
        refs = refs[2:]
    out_refs, (v_wide, acc, m) = refs[:-3], refs[-3:]
    sources, _, share, _ = kv_ref.shape
    size = sources * share
    heads, part, _ = here_ref.shape
    rows = 2 * part
    step = pl.program_id(0)
    sub = 256

    @pl.when(step == 0)
    def _():
        v_wide[:, :, HD:] = jnp.ones((heads, v_wide.shape[1], HD), BF)
        if first:
            m[...] = jnp.full(m.shape, LOWEST, F32)
            acc[...] = jnp.zeros(acc.shape, F32)
        else:
            m[...] = m_in[...]
            acc[...] = acc_in[...]

    def update(keys, count, gone):
        chains = [(head, at) for head in range(heads) for at in range(0, rows, sub)]
        scores = [
            lax.dot_general(
                (here_ref if at < part else there_ref)[head, at % part : at % part + sub],
                keys[head],
                (((1,), (1,)), ((), ())),
                preferred_element_type=F32,
            )
            for head, at in chains
        ]
        for (head, at), s in zip(chains, scores):
            if gone is not None:
                s = jnp.where(gone, LOWEST, s)
            m_old = m[head, at : at + sub]
            m_new = jnp.maximum(m_old, jnp.max(s, axis=1, keepdims=True))
            p = jnp.exp2(s - m_new[:, :1])
            alpha = jnp.exp2(m_old - m_new)
            acc[head, at : at + sub] = jnp.concatenate((alpha, alpha), axis=1) * acc[head, at : at + sub] + jnp.dot(
                p.astype(BF), v_wide[head, :count], preferred_element_type=F32
            )
            m[head, at : at + sub] = m_new

    def low(at):
        return spot[3] - (spot[0] * PLANE + step * sources + at) * length - begin

    touched = jnp.bool_(False)
    for at in range(sources):
        touched = touched | ((low(at) < share) & (low(at) + patch > 0))
    keys = [kv_ref[:, head].reshape(size, HD) for head in range(heads)]
    for head in range(heads):
        v_wide[head, :size, :HD] = kv_ref[:, heads + head].reshape(size, HD)

    @pl.when(touched)
    def _():
        column = lax.broadcasted_iota(jnp.int32, (1, size), 1)
        gone = jnp.zeros((1, size), jnp.int32)
        for at in range(sources):
            start = at * share + jnp.clip(low(at), 0, share)
            end = at * share + jnp.clip(low(at) + patch, 0, share)
            gone = jnp.where((column >= start) & (column < end), 1, gone)
        update(keys, size, gone > 0)

    @pl.when(jnp.logical_not(touched))
    def _():
        update(keys, size, None)

    @pl.when(step == pl.num_programs(0) - 1)
    def _():
        if fresh:
            count = fresh_ref.shape[1]
            for head in range(heads):
                v_wide[head, :count, :HD] = fresh_ref[heads + head]
            update([fresh_ref[head] for head in range(heads)], count, None)
        if last:
            for start, o_ref, lse_ref in ((0, *out_refs[:2]), (part, *out_refs[2:])):
                some = slice(start, start + part)
                for head in range(heads):
                    both = acc[head, some, :]
                    o_ref[head] = (both[:, :HD] / both[:, HD:]).astype(o_ref.dtype)
                    lse_ref[head] = jnp.transpose(m[head, some, :] + jnp.log2(both[:, HD:]))[:8, :]
        else:
            out_refs[0][...] = acc[...]
            out_refs[1][...] = m[...]


def attend(spot, q, stale, fresh, state, last, begin, length, patch, steps):
    heads, rows, _ = q[0].shape
    rows *= 2
    share = stale.shape[2]
    first = state is None
    whole = lambda shape: pl.BlockSpec(shape, lambda g, spot: (0,) * len(shape))
    sources = PLANE // steps
    inputs = [*q, stale]
    specs = [whole(q[0].shape), whole(q[1].shape), pl.BlockSpec((sources, 2 * heads, share, HD), lambda g, spot: (g, 0, 0, 0))]
    count = sources * share
    if fresh is not None:
        inputs.append(fresh)
        specs.append(whole(fresh.shape))
        count = max(count, fresh.shape[1])
    scratch = [pltpu.VMEM((heads, count, 2 * HD), BF), pltpu.VMEM((heads, rows, 2 * HD), F32), pltpu.VMEM((heads, rows, HD), F32)]
    if not first:
        inputs += list(state)
        specs += [whole(part.shape) for part in state]
    shapes = [((heads, rows, 2 * HD), F32), ((heads, rows, HD), F32)]
    if last:
        lse = ((heads, 8, rows // 2), F32)
        shapes = [((heads, rows // 2, HD), F32), lse, ((heads, rows // 2, HD), BF), lse]
    tokens = PLANE * share + (0 if fresh is None else fresh.shape[1])
    return pl.pallas_call(
        functools.partial(
            attend_kernel, fresh=fresh is not None, first=first, last=last, begin=begin, length=length, patch=patch
        ),
        grid_spec=pltpu.PrefetchScalarGridSpec(
            num_scalar_prefetch=1,
            grid=(steps,),
            in_specs=specs,
            out_specs=tuple(whole(shape) for shape, _ in shapes),
            scratch_shapes=scratch,
        ),
        out_shape=tuple(jax.ShapeDtypeStruct(*one) for one in shapes),
        compiler_params=pltpu.CompilerParams(vmem_limit_bytes=56 * 2**20),
        cost_estimate=pl.CostEstimate(
            flops=heads * rows * tokens * HD * 8, bytes_accessed=heads * tokens * HD * 4, transcendentals=heads * rows * tokens
        ),
    )(spot, *inputs)


def body(
    tokens,
    mod_shift,
    mod_scale,
    mod_gate,
    w_query,
    w_key,
    w_value,
    w_out,
    stale_keys,
    stale_values,
    patch_index,
):
    sections = lax.axis_size("section")
    me = lax.axis_index("seq")
    z, y, x = me // PLANE, me // NX % NY, me % NX
    rows, width = tokens.shape[1:]
    patch = COUNT * rows
    length = stale_keys.shape[1]
    spot = jnp.stack([z, y, x, patch_index[0] * patch]).astype(jnp.int32)
    planes = [list(range(plane * PLANE, (plane + 1) * PLANE)) for plane in range(NZ)]

    def stale_laid(begin, share, *deps):
        return lay_out(after(spot[:1], *deps) if deps else spot[:1], stale_keys[0], stale_values[0], begin, share)

    def stale_share(laid, *deps):
        laid = after(laid, *deps) if deps else laid
        return lax.all_to_all(laid, "seq", split_axis=0, concat_axis=0, tiled=True, axis_index_groups=planes)

    weights = []
    for w in (w_query, w_key, w_value):
        weights += [w[0], moved(w[0], dz=1)]

    inputs = tokens[0].astype(F32)
    meansq = jnp.mean(inputs * inputs, axis=-1, keepdims=True)
    normed = (inputs * lax.rsqrt(meansq + 1e-06) * (1.0 + mod_scale[0]) + mod_shift[0]).astype(BF)
    normed = lax.all_gather(normed, "seq", axis=0, tiled=True, axis_index_groups=planes)

    wide = width // NX
    w_slices, w_parts = [], []
    for k in range(NX):
        w_slices.append(lax.dynamic_slice(w_out[0], (0, (x + k) % NX * wide), (HD, wide)))
        w_parts.append(moved(w_slices[k], dx=k) if k else w_slices[k])
    q = project(spot, normed, weights[:2], LOG2E / HD**0.5)
    q_there = moved(q, dz=1)
    normed, weights, w_parts = lax.optimization_barrier((normed, weights, w_parts))
    w_plane = jnp.concatenate(w_parts, axis=0)

    early = 6 * rows
    stale_first = stale_share(stale_laid(0, early, *w_slices))
    stale_second = stale_share(stale_laid(early, length - early), normed)

    spot, q = lax.optimization_barrier((spot, q))
    fresh = project(spot, normed, weights[2:], 1.0)
    w_other = moved(after(w_plane, q_there), dz=1)
    tokens_behind = from_behind(after(tokens[0], q_there), "section", 1)
    gate_behind = from_behind(after(mod_gate, q_there), "section", 1)

    q = (q, q_there)
    state = attend(spot, q, stale_first, None, None, False, 0, length, patch, 4)
    fresh, w_other = lax.optimization_barrier((fresh, w_other))
    w_columns = jnp.concatenate((jnp.where(z == 0, w_plane, w_other), jnp.where(z == 0, w_other, w_plane)), axis=0)
    o_here, lse_here, o_there, lse_there = attend(spot, q, stale_second, fresh, state, True, early, length, patch, 4)

    o_got = moved(o_there, dz=1).astype(F32)
    lse_got = moved(lse_there, dz=1)
    part_here = (1.0 / (1.0 + jnp.exp2(lse_got - lse_here)))[:, 0, :, None]
    attended = (o_here * part_here + o_got * (1.0 - part_here)).astype(BF)
    attended = jnp.concatenate((attended[0], attended[1]), axis=1)

    along = [attended] + [moved(attended, dx=k) for k in range(1, NX)]
    gathered = jnp.concatenate([a[:, :HD] for a in along] + [a[:, HD:] for a in along], axis=1)
    partial = jnp.dot(gathered, w_columns, preferred_element_type=F32).astype(BF)
    band = NX * rows
    total = lax.dynamic_slice(partial, (y * band, 0), (band, wide)).astype(F32)
    for k in range(1, NY):
        part = lax.dynamic_slice(partial, ((y + k) % NY * band, 0), (band, wide))
        total = total + moved(part, dy=k).astype(F32)
    total = total.astype(BF)
    projected = jnp.zeros((rows, width), BF)
    for k in range(NX):
        part = onward(lax.dynamic_slice(total, ((x + k) % NX * rows, 0), (rows, wide)), sections, k)
        projected = lax.dynamic_update_slice(projected, part, (0, (x - k) % NX * wide))
    updated = tokens_behind.astype(F32) + gate_behind * projected.astype(F32)
    return updated.astype(BF)[None]


def solution(mesh):
    placed = (
        P("section", "seq", None),
        P("section", None),
        P("section", None),
        P("section", None),
        P("section", None, "seq"),
        P("section", None, "seq"),
        P("section", None, "seq"),
        P("section", "seq", None),
        P("section", "seq", None),
        P("section", "seq", None),
        P("section"),
    )
    return jax.shard_map(
        body, mesh=mesh, in_specs=placed, out_specs=P("section", "seq", None), check_vma=False
    )
```
